32 devices in a mesh: dp: 2 (over y), seq: 16 (over z, x, core).
Axes of the slice: x: 2, y: 2, z: 4, core: 2. Of those that a mesh axis runs over, the one named last changes fastest.
Arguments:
- tokens: bfloat16 [2, 4096, 4096], P('dp', 'seq'), may hold values from -6 to 6
- queries: bfloat16 [2, 4096, 128], P('dp', 'seq'), may hold values from -6 to 6
- key_vectors: bfloat16 [2, 4096, 128], P('dp', 'seq'), may hold values from -6 to 6
- doc_position: int32 [2, 4096], P('dp', 'seq'), may hold values from 0 to 4095, as said below
- value_scores: float32 [2, 4096, 4], P('dp', 'seq'), may hold values from 0.1 to 1
- value_experts: int32 [2, 4096, 2], P('dp', 'seq'), may hold values from 0 to 3, all different within a row
- output_scores: float32 [2, 4096, 4], P('dp', 'seq'), may hold values from 0.1 to 1
- output_experts: int32 [2, 4096, 2], P('dp', 'seq'), may hold values from 0 to 3, all different within a row
- value_panels: bfloat16 [4096, 512], P('seq'), may hold values from -0.09375 to 0.09375
- output_panels: bfloat16 [4096, 512], P('seq'), may hold values from -3 to 3
- cotangent: bfloat16 [2, 4096, 4096], P('dp', 'seq'), may hold values from -0.4375 to 0.4375
Outputs:
- layer_output: bfloat16 [2, 4096, 4096], P('dp', 'seq')
- grad_tokens: bfloat16 [2, 4096, 4096], P('dp', 'seq')
- grad_queries: bfloat16 [2, 4096, 128], P('dp', 'seq')
- grad_keys: bfloat16 [2, 4096, 128], P('dp', 'seq')
- grad_value: float32 [4096, 512], P('seq')
- grad_output: float32 [4096, 512], P('seq')
The draws below stay inside these ranges and needn't reach their ends.
Inputs may be any that keep to these rules, and one draw needn't show every extreme that they name: doc_position[b, i] is i minus the first position of the document that holds position i; position 0 starts a document in every sequence; sequence 0 is one document; every other sequence holds one to four documents.
All inputs are finite; a program needn't handle non-finite values.
Results may differ from the reference program's by a relative error of at most 0.035.
Values may be sent and summed in bfloat16 or wider, within the bound.
A program may use at most 128 MiB of HBM per device.

```python
import math
import jax
import jax.numpy as jnp
from jax import lax

D = 4096
DH = 128
EXPERTS = 4
TOPK = 2
TOK_DEV = 256
LENGTH = 4096
BATCH = 2
N_SEQ = 16


def joint_draw(key):
    folded = jax.random.fold_in(key, 17)
    streams = jax.random.split(folded, 2)
    full_shape = (BATCH, LENGTH, DH)
    query_vals = jnp.clip(1.4 * jax.random.normal(streams[0], full_shape, jnp.float32), -6.0, 6.0)
    key_vals = jnp.clip(1.4 * jax.random.normal(streams[1], full_shape, jnp.float32), -6.0, 6.0)
    return (query_vals, key_vals)


def draw_queries(key, part):
    return joint_draw(key)[0].astype(jnp.bfloat16)


def draw_key_vectors(key, part):
    return joint_draw(key)[1].astype(jnp.bfloat16)


def draw_doc_position(key, part):
    boundaries = jax.random.randint(jax.random.fold_in(key, 5), (BATCH, 3), 1, LENGTH)
    positions = jnp.arange(LENGTH, dtype=jnp.int32)
    starts_doc = jnp.any(positions[None, :, None] == boundaries[:, None, :], axis=2)
    starts_doc = starts_doc & (jnp.arange(BATCH, dtype=jnp.int32)[:, None] > 0)
    starts_doc = starts_doc | (positions[None, :] == 0)
    start_marks = jnp.where(starts_doc, positions[None, :], 0)
    last_start = lax.cummax(start_marks, axis=1)
    return (positions[None, :] - last_start).astype(jnp.int32)


def spiked(values, own_key, source, target, blocks, factor):
    owner, partner = [(jnp.arange(values.shape[axis_at]) // (values.shape[axis_at] // blocks)).reshape([-1 if axis == axis_at else 1 for axis in range(values.ndim)]) for axis_at in (source, target)]
    chosen = jax.random.permutation(own_key, blocks)[partner]
    strong = (owner == chosen) | (owner == (partner + blocks // 2) % blocks)
    return jnp.where(strong, factor * values, values)


def level_of(stream_key, shape, cuts, low, top_value):
    factor_of, own = 1.0, jax.random.fold_in(stream_key, 6)
    for position, parts in cuts:
        heights = jnp.exp(jax.random.uniform(jax.random.fold_in(own, position), (parts,), jnp.float32, low / len(cuts), top_value / len(cuts)))
        factor_of = factor_of * jnp.repeat(heights, shape[position] // parts).reshape([-1 if axis == position else 1 for axis in range(len(shape))])
    return factor_of


def different_ones(own_key, rows, amount, top, lift):
    ranking = jax.random.permutation(jax.random.fold_in(own_key, 1), amount)
    boost = ranking
    for power in range(3):
        boost = boost * boost // amount
    boost = boost * lift // amount
    lots = jax.random.randint(jax.random.fold_in(own_key, 2), (rows, amount), 0, 4096) + boost
    holders = jax.random.permutation(jax.random.fold_in(own_key, 3), rows)[jnp.arange(amount) % rows]
    lots = jnp.where(jnp.arange(rows)[:, None] == holders[None, :], 1 << 14, lots)
    merit = lots * amount + jnp.arange(amount)
    return lax.top_k(merit.astype(jnp.int32), top)[1].astype(jnp.int32)


def centred(key, extent, scale, bound, pieces=(), kind=jnp.bfloat16):
    drawn = scale * jax.random.normal(key, extent, jnp.float32)
    if pieces:
        drawn = drawn * level_of(key, extent, pieces, -0.22, 0.18)
    return jnp.clip(drawn, -bound, bound).astype(kind)


def noise_with(stream_key, shape, scale, reach, cuts, heavy, kind=jnp.bfloat16):
    result = scale * jax.random.normal(stream_key, shape, jnp.float32)
    if cuts:
        result = result * level_of(stream_key, shape, cuts, -0.22, 0.18)
    return jnp.clip(spiked(result, jax.random.fold_in(stream_key, 3), *heavy), -reach, reach).astype(kind)


def setup_inputs(seed: int = 0) -> dict:
    key_list = jax.random.split(jax.random.key(seed), 12)
    return {
        "tokens": noise_with(key_list[0], (BATCH, LENGTH, D), 1.0, 6.0, ((0, 2), (1, 16)), (1, 2, 16, 2.0)),
        "queries": draw_queries(jax.random.fold_in(key_list[11], 71), 0),
        "key_vectors": draw_key_vectors(jax.random.fold_in(key_list[11], 71), 0),
        "doc_position": draw_doc_position(jax.random.fold_in(key_list[11], 71), 0),
        "value_scores": jnp.clip(jnp.exp(math.log(1.0) - 2.3025851 * jax.random.uniform(key_list[4], (BATCH, LENGTH, EXPERTS), jnp.float32) ** level_of(key_list[4], (BATCH, LENGTH, EXPERTS), ((0, 2), (1, 16)), -0.2, 0.2)), 0.1, 1.0),
        "value_experts": different_ones(key_list[5], BATCH * LENGTH, EXPERTS, TOPK, 4096).reshape((BATCH, LENGTH, TOPK)),
        "output_scores": jnp.clip(jnp.exp(math.log(1.0) - 2.3025851 * jax.random.uniform(key_list[6], (BATCH, LENGTH, EXPERTS), jnp.float32) ** level_of(key_list[6], (BATCH, LENGTH, EXPERTS), ((0, 2), (1, 16)), -0.2, 0.2)), 0.1, 1.0),
        "output_experts": different_ones(key_list[7], BATCH * LENGTH, EXPERTS, TOPK, 4096).reshape((BATCH, LENGTH, TOPK)),
        "value_panels": centred(key_list[8], (D, EXPERTS * DH), D ** -0.5, 0.09375, ((0, 16),)),
        "output_panels": centred(key_list[9], (D, EXPERTS * DH), 0.5, 3.0, ((0, 16),)),
        "cotangent": noise_with(key_list[10], (BATCH, LENGTH, D), 0.05, 0.4375, ((0, 2), (1, 16)), (1, 2, 16, 2.0)),
    }


def expert_gates(scores, chosen):
    chosen_hit = jnp.any(chosen[:, :, None] == jnp.arange(EXPERTS, dtype=jnp.int32)[None, None, :], axis=1)
    return jnp.where(chosen_hit, scores.astype(jnp.float32), jnp.float32(0.0))


def one_sequence(tok_seq, query_seq, key_seq, position_seq, value_scores, value_experts, output_scores, output_experts, value_panels, output_panels, grad_seq):
    value_gate = expert_gates(value_scores, value_experts)
    output_gate = expert_gates(output_scores, output_experts)
    projection = jnp.dot(tok_seq, value_panels, preferred_element_type=jnp.float32)
    value_vec = jnp.sum(projection.reshape(LENGTH, EXPERTS, DH) * value_gate[:, :, None], axis=1).astype(jnp.bfloat16)
    pulled = jnp.dot(grad_seq, output_panels, preferred_element_type=jnp.float32)
    dattended = jnp.sum(pulled.reshape(LENGTH, EXPERTS, DH) * output_gate[:, :, None], axis=1).astype(jnp.bfloat16)
    block_rows = math.gcd(LENGTH, 512)
    block_count = LENGTH // block_rows
    key_index = jnp.arange(LENGTH, dtype=jnp.int32)
    score_scale = DH ** -0.5

    def attend_block(carried, offset):
        dkey_sum, dvalue_sum = carried
        query_block = lax.dynamic_slice_in_dim(query_seq, offset, block_rows, 0)
        limit_block = lax.dynamic_slice_in_dim(position_seq, offset, block_rows, 0)
        dattended_block = lax.dynamic_slice_in_dim(dattended, offset, block_rows, 0)
        query_index = offset + jnp.arange(block_rows, dtype=jnp.int32)
        visible = (key_index[None, :] <= query_index[:, None]) & (query_index[:, None] - key_index[None, :] <= limit_block[:, None])
        scores = jnp.dot(query_block, key_seq.T, preferred_element_type=jnp.float32) * score_scale
        masked = jnp.where(visible, scores, -jnp.inf)
        row_max = jnp.max(masked, axis=1)
        log_total = row_max + jnp.log(jnp.sum(jnp.exp(masked - row_max[:, None]), axis=1))
        attn_prob = jnp.exp(masked - log_total[:, None])
        prob_low = attn_prob.astype(jnp.bfloat16)
        attended = jnp.dot(prob_low, value_vec, preferred_element_type=jnp.float32).astype(jnp.bfloat16)
        row_delta = jnp.sum(dattended_block.astype(jnp.float32) * attended.astype(jnp.float32), axis=1)
        dweights = jnp.dot(dattended_block, value_vec.T, preferred_element_type=jnp.float32)
        dscores = (attn_prob * (dweights - row_delta[:, None])).astype(jnp.bfloat16)
        grad_query = (jnp.dot(dscores, key_seq, preferred_element_type=jnp.float32) * score_scale).astype(jnp.bfloat16)
        dkey_sum = dkey_sum + jnp.dot(dscores.T, query_block, preferred_element_type=jnp.float32) * score_scale
        dvalue_sum = dvalue_sum + jnp.dot(prob_low.T, dattended_block, preferred_element_type=jnp.float32)
        return (dkey_sum, dvalue_sum), (attended, grad_query)

    offsets = jnp.arange(block_count, dtype=jnp.int32) * block_rows
    zeros_acc = jnp.zeros((LENGTH, DH), jnp.float32)
    (dkey_sum, dvalue_sum), (attended, grad_query) = lax.scan(attend_block, (zeros_acc, zeros_acc), offsets)
    attended = attended.reshape(LENGTH, DH)
    grad_query = grad_query.reshape(LENGTH, DH)
    expanded = (output_gate[:, :, None] * attended.astype(jnp.float32)[:, None, :]).reshape(LENGTH, EXPERTS * DH).astype(jnp.bfloat16)
    layer_output = jnp.dot(expanded, output_panels.T, preferred_element_type=jnp.float32).astype(jnp.bfloat16)
    dvalue = dvalue_sum.astype(jnp.bfloat16)
    value_grad = (value_gate[:, :, None] * dvalue.astype(jnp.float32)[:, None, :]).reshape(LENGTH, EXPERTS * DH).astype(jnp.bfloat16)
    grad_tok = jnp.dot(value_grad, value_panels.T, preferred_element_type=jnp.float32).astype(jnp.bfloat16)

    def weight_block(carried, block_index):
        offset = block_index * TOK_DEV
        tok_slice = lax.dynamic_slice_in_dim(tok_seq, offset, TOK_DEV, 0)
        grad_slice = lax.dynamic_slice_in_dim(grad_seq, offset, TOK_DEV, 0)
        value_slice = lax.dynamic_slice_in_dim(value_grad, offset, TOK_DEV, 0)
        expanded_slice = lax.dynamic_slice_in_dim(expanded, offset, TOK_DEV, 0)
        term_value = jnp.dot(tok_slice.T, value_slice, preferred_element_type=jnp.float32)
        term_output = jnp.dot(grad_slice.T, expanded_slice, preferred_element_type=jnp.float32)
        term_value = lax.optimization_barrier(term_value.astype(jnp.bfloat16)).astype(jnp.float32)
        term_output = lax.optimization_barrier(term_output.astype(jnp.bfloat16)).astype(jnp.float32)
        return (carried[0] + term_value, carried[1] + term_output), None

    weight_zero = jnp.zeros((D, EXPERTS * DH), jnp.float32)
    (grad_value, grad_output), _ = lax.scan(weight_block, (weight_zero, weight_zero), jnp.arange(N_SEQ, dtype=jnp.int32))
    return layer_output, grad_tok, grad_query, dkey_sum.astype(jnp.bfloat16), grad_value, grad_output


def reference(tokens, queries, key_vectors, doc_position, value_scores, value_experts, output_scores, output_experts, value_panels, output_panels, cotangent):
    outputs_list = []
    grad_tok_list = []
    grad_query_list = []
    grad_key_list = []
    grad_value = jnp.zeros((D, EXPERTS * DH), jnp.float32)
    grad_output = jnp.zeros((D, EXPERTS * DH), jnp.float32)
    for seq_index in range(BATCH):
        results = one_sequence(tokens[seq_index], queries[seq_index], key_vectors[seq_index], doc_position[seq_index], value_scores[seq_index], value_experts[seq_index], output_scores[seq_index], output_experts[seq_index], value_panels, output_panels, cotangent[seq_index])
        outputs_list.append(results[0])
        grad_tok_list.append(results[1])
        grad_query_list.append(results[2])
        grad_key_list.append(results[3])
        grad_value = grad_value + results[4]
        grad_output = grad_output + results[5]
    return (jnp.stack(outputs_list), jnp.stack(grad_tok_list), jnp.stack(grad_query_list), jnp.stack(grad_key_list), grad_value, grad_output)
```

```python
import functools

import jax
import jax.numpy as jnp
from jax import lax
from jax.experimental import pallas as pl
from jax.experimental.pallas import tpu as pltpu
from jax.sharding import PartitionSpec as P

MESH = pl.DeviceIdType.MESH


class Place:
    def __init__(self, lines, crosses):
        index = lax.axis_index("seq")
        self.lines, self.crosses = lines, crosses
        self.dp = lax.axis_index("dp")
        self.a = index // (2 * crosses)
        self.b = (index // 2) % crosses
        self.c = index % 2
        self.side = self.dp % 2
        self.mate = self.dp + 1 - 2 * self.side

    def at(self, a=None, b=None, c=None, dp=None):
        a = self.a if a is None else a
        b = self.b if b is None else b
        c = self.c if c is None else c
        dp = self.dp if dp is None else dp
        return (dp, (a * self.crosses + b) * 2 + c)

    def others(self):
        return [lax.rem(self.b + k, self.crosses) for k in range(1, self.crosses)]

    def greet(self, paired):
        barrier = pltpu.get_barrier_semaphore()

        def hail(device):
            pl.semaphore_signal(barrier, inc=1, device_id=device, device_id_type=MESH)

        @pl.when(self.a > 0)
        def _():
            hail(self.at(a=self.a - 1))

        @pl.when(self.a < self.lines - 1)
        def _():
            hail(self.at(a=self.a + 1))

        for q in self.others():
            hail(self.at(b=q))
        hail(self.at(c=1 - self.c))
        if paired:
            hail(self.at(dp=self.mate))

    def await_greetings(self, paired):
        barrier = pltpu.get_barrier_semaphore()

        ends = jnp.where(self.a > 0, 1, 0) + jnp.where(self.a < self.lines - 1, 1, 0)
        pl.semaphore_wait(barrier, ends + self.crosses + (1 if paired else 0))

    def ring(self, t):
        if t == 0:
            return [(self.a, 0, None)]
        up, down = self.a + t, self.a - t
        return [(down, -1, down >= 0), (up, 1, up < self.lines)]


def only(flag, action):
    if flag is None:
        action()
    else:
        pl.when(flag)(action)


def both(left, right):
    if left is None:
        return right
    return left if right is None else jnp.logical_and(left, right)


def split_rows(rows):
    alone = rows * 3 // 8
    return rows - alone, alone


def gather_kernel(lines, crosses, paired, *refs):
    count = len(paired)
    owns, outs = refs[:count], refs[count : 2 * count]
    sems = refs[2 * count : 3 * count]
    local_sem = refs[3 * count]
    here = Place(lines, crosses)
    pieces = lines * crosses
    zs0, zr0 = 0, 2 * lines
    xs0 = 3 * lines
    xr0, ys0, yr0, cs0, cr0 = (xs0 + k * pieces for k in range(1, 6))
    any_pair = any(paired)

    def span(item, p, q, c, part):
        rows = owns[item].shape[0]
        start = ((p * crosses + q) * 2 + c) * rows
        if part == "whole" or not paired[item]:
            return outs[item].at[pl.ds(pl.multiple_of(start, 16), rows)]
        carried, alone = split_rows(rows)
        if part == "carried":
            return outs[item].at[
                pl.ds(pl.multiple_of(start + alone * here.side, 16), carried)
            ]
        side = here.side if part == "mine" else 1 - here.side
        return outs[item].at[
            pl.ds(pl.multiple_of(start + carried * side, 16), alone)
        ]

    def move(item, ref, send, recv, device):
        return pltpu.make_async_remote_copy(
            src_ref=ref,
            dst_ref=ref,
            send_sem=sems[item].at[send],
            recv_sem=sems[item].at[recv],
            device_id=device,
            device_id_type=MESH,
        )

    def along(item, p, step):
        return move(
            item, span(item, p, here.b, here.c, "carried"),
            zs0 + 2 * p + (1 if step > 0 else 0), zr0 + p, here.at(a=here.a + step),
        )

    def across(item, p, q):
        return move(
            item, span(item, p, here.b, here.c, "carried"),
            xs0 + p * crosses + q, xr0 + p * crosses + here.b, here.at(b=q),
        )

    def crossed(item, p, q):
        return move(
            item, span(item, p, q, here.c, "carried"),
            xs0 + p * crosses + q, xr0 + p * crosses + q, here.at(b=q),
        )

    def to_mate(item, p, q, part="mine"):
        return move(
            item, span(item, p, q, here.c, part),
            ys0 + p * crosses + q, yr0 + p * crosses + q, here.at(dp=here.mate),
        )

    def to_core(item, p, q, c):
        return move(
            item, span(item, p, q, c, "whole"),
            cs0 + p * crosses + q, cr0 + p * crosses + q, here.at(c=1 - here.c),
        )

    def pass_on(item, p, q):
        if paired[item]:
            to_mate(item, p, q).start()
        else:
            to_core(item, p, q, here.c).start()

    here.greet(any_pair)
    copies = [
        pltpu.make_async_copy(
            owns[item], span(item, here.a, here.b, here.c, "whole"), local_sem.at[item]
        )
        for item in range(count)
    ]
    for copy in copies:
        copy.start()
    for copy in copies:
        copy.wait()
    here.await_greetings(any_pair)

    up_ok, down_ok = here.a < lines - 1, here.a > 0

    def send_line(item, p, step):
        only(up_ok if step > 0 else down_ok, lambda: along(item, p, step).start())

    for item in range(count):
        send_line(item, here.a, 1)
        send_line(item, here.a, -1)
        for q in here.others():
            across(item, here.a, q).start()
        to_core(item, here.a, here.b, here.c).start()

    def take_across(t):
        for p, _, ok in here.ring(t):

            def action(p=p):
                for item in range(count):
                    for q in here.others():
                        crossed(item, p, q).wait_recv()
                        pass_on(item, p, q)

            only(ok, action)

    def take_mate(t):
        for p, _, ok in here.ring(t):

            def action(p=p):
                for item in range(count):
                    if paired[item]:
                        for q in here.others() + ([] if t == 0 else [here.b]):
                            to_mate(item, p, q, "theirs").wait_recv()
                            to_core(item, p, q, here.c).start()

            only(ok, action)

    for t in range(1, lines):
        for p, step, ok in here.ring(t):

            def action(p=p, step=step):
                for item in range(count):
                    along(item, p, -step).wait_recv()
                    send_line(item, p, -step)
                    for q in here.others():
                        across(item, p, q).start()
                    pass_on(item, p, here.b)

            only(ok, action)
        take_across(t - 1)
        if t >= 2:
            take_mate(t - 2)
    take_across(lines - 1)
    if lines >= 2:
        take_mate(lines - 2)
    take_mate(lines - 1)

    for p in range(lines):
        for q in range(crosses):
            for item in range(count):
                to_core(item, p, q, 1 - here.c).wait_recv()
                to_core(item, p, q, here.c).wait_send()
                if paired[item]:
                    pl.when(jnp.logical_or(p != here.a, q != here.b))(
                        lambda item=item, p=p, q=q: to_mate(item, p, q).wait_send()
                    )
    for p in range(lines):
        for item in range(count):
            for q in here.others():
                across(item, p, q).wait_send()
            pl.when(jnp.logical_and(up_ok, p <= here.a))(
                lambda item=item, p=p: along(item, p, 1).wait_send()
            )
            pl.when(jnp.logical_and(down_ok, p >= here.a))(
                lambda item=item, p=p: along(item, p, -1).wait_send()
            )


def layout(size):
    lines = 4 if size % 8 == 0 else 1
    return lines, size // (2 * lines)


def gather(arrays, paired, size, collective_id):
    lines, crosses = layout(size)
    count = len(arrays)
    return pl.pallas_call(
        functools.partial(gather_kernel, lines, crosses, tuple(paired)),
        out_shape=[
            jax.ShapeDtypeStruct((size * x.shape[0],) + x.shape[1:], x.dtype) for x in arrays
        ],
        in_specs=[pl.BlockSpec(memory_space=pl.ANY)] * count,
        out_specs=[pl.BlockSpec(memory_space=pl.ANY)] * count,
        scratch_shapes=[
            pltpu.SemaphoreType.DMA((3 * lines + 6 * lines * crosses,)) for _ in range(count)
        ]
        + [pltpu.SemaphoreType.DMA((count,))],
        compiler_params=pltpu.CompilerParams(
            collective_id=collective_id, has_side_effects=True
        ),
    )(*arrays)


def reduce_kernel(lines, crosses, paired, x_ref, out_ref, total, core_in, mate_in, cross_in,
                  line_in, last_in, sems):
    here = Place(lines, crosses)
    pieces = lines * crosses
    rows = out_ref.shape[0]
    carried, alone = split_rows(rows) if paired else (rows, 0)
    cs0, cr0, ys0, yr0, xs0, xr0 = (k * pieces for k in range(6))
    zs0 = 6 * pieces
    zr0, fs, fr = zs0 + lines, zs0 + 3 * lines, zs0 + 3 * lines + 1
    first = pl.ds(pl.multiple_of(alone * here.side, 16), carried) if paired else pl.ds(0, rows)
    mine = pl.ds(pl.multiple_of(carried * here.side, 16), alone)
    theirs = pl.ds(pl.multiple_of(carried * (1 - here.side), 16), alone)

    def move(src, dst, send, recv, device):
        return pltpu.make_async_remote_copy(
            src_ref=src, dst_ref=dst, send_sem=sems.at[send], recv_sem=sems.at[recv],
            device_id=device, device_id_type=MESH,
        )

    def slot(p, q):
        return p * crosses + q

    def piece(p, q, c):
        return pl.ds(pl.multiple_of(((p * crosses + q) * 2 + c) * rows, 16), rows)

    def to_core(p, q):
        k = slot(p, q)
        return move(x_ref.at[piece(p, q, 1 - here.c)], core_in.at[k], cs0 + k, cr0 + k,
                    here.at(c=1 - here.c))

    def to_mate(p, q):
        k = slot(p, q)
        return move(total.at[k, theirs], mate_in.at[k], ys0 + k, yr0 + k,
                    here.at(dp=here.mate))

    def across(p, q):
        return move(total.at[slot(p, q), first], cross_in.at[slot(p, here.b)],
                    xs0 + slot(p, q), xr0 + slot(p, here.b), here.at(b=q))

    def crossed(p, q):
        return move(total.at[slot(p, q), first], cross_in.at[slot(p, q)],
                    xs0 + slot(p, q), xr0 + slot(p, q), here.at(b=q))

    def along(p, step):
        k = 2 * p + (0 if step > 0 else 1)
        return move(total.at[slot(p, here.b), first], line_in.at[k], zs0 + p, zr0 + k,
                    here.at(a=here.a + step))

    def final():
        return move(total.at[slot(here.a, here.b), first], last_in, fs, fr,
                    here.at(dp=here.mate))

    here.greet(paired)
    here.await_greetings(paired)
    order = [(t, q) for t in range(lines - 1, -1, -1) for q in here.others() + [here.b]]
    for t, q in order:
        for p, _, ok in here.ring(t):
            only(ok, lambda p=p, q=q: to_core(p, q).start())
    for t, q in order:
        for p, _, ok in here.ring(t):

            def join(p=p, q=q):
                k = slot(p, q)
                to_core(p, q).wait_recv()
                total[k] = x_ref[piece(p, q, here.c)] + core_in[k]
                if paired:
                    to_mate(p, q).start()

            only(ok, join)
    for t in range(lines - 1, -1, -1):
        for q in here.others():
            for p, _, ok in here.ring(t):

                def cross(p=p, q=q):
                    k = slot(p, q)
                    if paired:
                        to_mate(p, q).wait_recv()
                        total[k, mine] = total[k, mine] + mate_in[k]
                    across(p, q).start()

                only(ok, cross)
        for p, _, ok in here.ring(t):

            def fold(p=p):
                if paired:
                    k = slot(p, here.b)
                    to_mate(p, here.b).wait_recv()
                    total[k, mine] = total[k, mine] + mate_in[k]

            only(ok, fold)
    for t in range(lines - 1, -1, -1):
        for p, step, ok in here.ring(t):

            def run(p=p, step=step):
                k = slot(p, here.b)
                for q in here.others():
                    crossed(p, q).wait_recv()
                    total[k, first] = total[k, first] + cross_in[slot(p, q)]

                def add(side):
                    along(p, 1 if side == 0 else -1).wait_recv()
                    total[k, first] = total[k, first] + line_in[2 * p + side]

                if step >= 0:
                    pl.when(here.a > 0)(lambda: add(0))
                if step <= 0:
                    pl.when(here.a < lines - 1)(lambda: add(1))
                if step != 0:
                    along(p, step).start()

            only(ok, run)

    k = slot(here.a, here.b)
    if paired:
        final().start()
        final().wait_recv()
        out_ref[mine] = total[k, mine].astype(out_ref.dtype)
        their_at = pl.multiple_of(alone * (1 - here.side) * 0 + (carried - alone) * (1 - here.side), 16)
        out_ref[theirs] = last_in[pl.ds(their_at, alone)].astype(out_ref.dtype)
        middle = carried - alone
        shared_at = pl.multiple_of(alone * here.side, 16)
        out_ref[pl.ds(alone, middle)] = total[k, pl.ds(alone, middle)].astype(
            out_ref.dtype
        ) + last_in[pl.ds(shared_at, middle)].astype(out_ref.dtype)
        final().wait_send()
    else:
        out_ref[...] = total[k].astype(out_ref.dtype)
    for p in range(lines):
        for q in range(crosses):
            to_core(p, q).wait_send()
            if paired:
                to_mate(p, q).wait_send()
        for q in here.others():
            across(p, q).wait_send()
        pl.when(p > here.a)(lambda p=p: along(p, 1).wait_send())
        pl.when(p < here.a)(lambda p=p: along(p, -1).wait_send())


def reduce_scatter(x, paired, size, out_dtype, collective_id):
    lines, crosses = layout(size)
    pieces = lines * crosses
    rows, width = x.shape[0] // size, x.shape[1]
    carried, alone = split_rows(rows) if paired else (rows, 16)
    kind = x.dtype
    return pl.pallas_call(
        functools.partial(reduce_kernel, lines, crosses, paired),
        out_shape=jax.ShapeDtypeStruct((rows, width), out_dtype),
        in_specs=[pl.BlockSpec(memory_space=pltpu.VMEM)],
        out_specs=pl.BlockSpec(memory_space=pltpu.VMEM),
        scratch_shapes=[
            pltpu.VMEM((pieces, rows, width), kind),
            pltpu.VMEM((pieces, rows, width), kind),
            pltpu.VMEM((pieces, alone, width), kind),
            pltpu.VMEM((pieces, carried, width), kind),
            pltpu.VMEM((2 * lines, carried, width), kind),
            pltpu.VMEM((carried, width), kind),
            pltpu.SemaphoreType.DMA((6 * pieces + 3 * lines + 2,)),
        ],
        compiler_params=pltpu.CompilerParams(
            collective_id=collective_id, has_side_effects=True,
            vmem_limit_bytes=56 * 1024 * 1024,
        ),
    )(x)


def expert_gates(scores, chosen, experts):
    chosen_hit = chosen[:, :, None] == lax.iota(jnp.int32, experts)[None, None, :]
    return jnp.where(jnp.any(chosen_hit, axis=1), scores, jnp.float32(0.0))


def contract_last(left, right):
    return lax.dot_general(
        left, right, (((1,), (1,)), ((), ())), preferred_element_type=jnp.float32
    )


def contract_first(left, right):
    return lax.dot_general(
        left, right, (((0,), (0,)), ((), ())), preferred_element_type=jnp.float32
    )


def body(
    tokens,
    queries,
    key_vectors,
    doc_position,
    value_scores,
    value_experts,
    output_scores,
    output_experts,
    value_panels,
    output_panels,
    cotangent,
):
    tok_block = tokens[0]
    query_block = queries[0]
    own_keys = key_vectors[0]
    positions = doc_position[0]
    grad_rows = cotangent[0]
    tok_rows = tok_block.shape[0]
    head_size = query_block.shape[1]
    experts = value_scores.shape[2]
    panel_width = value_panels.shape[1]
    value_gate = expert_gates(value_scores[0], value_experts[0], experts)
    output_gate = expert_gates(output_scores[0], output_experts[0], experts)
    size = lax.axis_size("seq")
    pair_count = lax.axis_size("dp")
    keys_all, value_full, output_full = gather(
        [own_keys, value_panels, output_panels], [False, True, True], size, 0
    )
    projection = jnp.dot(tok_block, value_full, preferred_element_type=jnp.float32)
    value_vec = jnp.sum(
        projection.reshape(tok_rows, experts, head_size) * value_gate[:, :, None], axis=1
    ).astype(jnp.bfloat16)
    (values_all,) = gather([value_vec], [False], size, 1)
    length = keys_all.shape[0]
    score_scale = head_size ** (-0.5)
    query_index = lax.axis_index("seq") * tok_rows + lax.iota(jnp.int32, tok_rows)
    key_index = lax.iota(jnp.int32, length)
    visible = (key_index[None, :] <= query_index[:, None]) & (
        query_index[:, None] - key_index[None, :] <= positions[:, None]
    )
    masked = jnp.where(visible, contract_last(query_block, keys_all) * score_scale, -jnp.inf)
    row_max = jnp.max(masked, axis=1)
    log_total = row_max + jnp.log(jnp.sum(jnp.exp(masked - row_max[:, None]), axis=1))
    attn_prob = jnp.exp(masked - log_total[:, None])
    prob_low = attn_prob.astype(jnp.bfloat16)
    attended = jnp.dot(prob_low, values_all, preferred_element_type=jnp.float32).astype(
        jnp.bfloat16
    )
    expanded = (
        (output_gate[:, :, None] * attended.astype(jnp.float32)[:, None, :])
        .reshape(tok_rows, panel_width)
        .astype(jnp.bfloat16)
    )
    layer_output = contract_last(expanded, output_full).astype(jnp.bfloat16)
    pulled = jnp.dot(grad_rows, output_full, preferred_element_type=jnp.float32)
    dattended = jnp.sum(
        pulled.reshape(tok_rows, experts, head_size) * output_gate[:, :, None], axis=1
    ).astype(jnp.bfloat16)
    row_delta = jnp.sum(dattended.astype(jnp.float32) * attended.astype(jnp.float32), axis=1)
    dweights = contract_last(dattended, values_all)
    dscores = (attn_prob * (dweights - row_delta[:, None])).astype(jnp.bfloat16)
    grad_queries = (
        jnp.dot(dscores, keys_all, preferred_element_type=jnp.float32) * score_scale
    ).astype(jnp.bfloat16)
    key_term = contract_first(dscores, query_block) * score_scale
    value_term = contract_first(prob_low, dattended)
    own_sums = reduce_scatter(
        jnp.concatenate([key_term, value_term], axis=1).astype(jnp.bfloat16),
        False, size, jnp.bfloat16, 2,
    )
    grad_keys, dvalue = own_sums[:, :head_size], own_sums[:, head_size:]
    value_grad = (
        (value_gate[:, :, None] * dvalue.astype(jnp.float32)[:, None, :])
        .reshape(tok_rows, panel_width)
        .astype(jnp.bfloat16)
    )
    grad_tokens = contract_last(value_grad, value_full).astype(jnp.bfloat16)
    term_value = contract_first(tok_block, value_grad)
    term_output = contract_first(grad_rows, expanded)
    summed = reduce_scatter(
        jnp.concatenate([term_value, term_output], axis=1).astype(jnp.bfloat16),
        True, size, jnp.float32, 3,
    )
    if pair_count > 2:
        summed = lax.psum(summed * 0.5, "dp")
    return (
        layer_output[None],
        grad_tokens[None],
        grad_queries[None],
        grad_keys[None],
        summed[:, :panel_width],
        summed[:, panel_width:],
    )


def solution(mesh):
    in_specs = (
        P("dp", "seq", None),
        P("dp", "seq", None),
        P("dp", "seq", None),
        P("dp", "seq"),
        P("dp", "seq", None),
        P("dp", "seq", None),
        P("dp", "seq", None),
        P("dp", "seq", None),
        P("seq", None),
        P("seq", None),
        P("dp", "seq", None),
    )
    out_specs = (
        P("dp", "seq", None),
        P("dp", "seq", None),
        P("dp", "seq", None),
        P("dp", "seq", None),
        P("seq", None),
        P("seq", None),
    )
    return jax.shard_map(body, mesh=mesh, in_specs=in_specs, out_specs=out_specs, check_vma=False)
```

```python
import functools

import jax
import jax.numpy as jnp
from jax import lax
from jax.experimental import pallas as pl
from jax.experimental.pallas import tpu as pltpu
from jax.sharding import PartitionSpec as P

MESH = pl.DeviceIdType.MESH


class Place:
    def __init__(self, lines, crosses):
        index = lax.axis_index("seq")
        self.lines, self.crosses = lines, crosses
        self.dp = lax.axis_index("dp")
        self.a = index // (2 * crosses)
        self.b = (index // 2) % crosses
        self.c = index % 2
        self.side = self.dp % 2
        self.mate = self.dp + 1 - 2 * self.side

    def at(self, a=None, b=None, c=None, dp=None):
        a = self.a if a is None else a
        b = self.b if b is None else b
        c = self.c if c is None else c
        dp = self.dp if dp is None else dp
        return (dp, (a * self.crosses + b) * 2 + c)

    def others(self):
        return [lax.rem(self.b + k, self.crosses) for k in range(1, self.crosses)]

    def greet(self, paired):
        barrier = pltpu.get_barrier_semaphore()

        def hail(device):
            pl.semaphore_signal(barrier, inc=1, device_id=device, device_id_type=MESH)

        @pl.when(self.a > 0)
        def _():
            hail(self.at(a=self.a - 1))

        @pl.when(self.a < self.lines - 1)
        def _():
            hail(self.at(a=self.a + 1))

        for q in self.others():
            hail(self.at(b=q))
        hail(self.at(c=1 - self.c))
        if paired:
            hail(self.at(dp=self.mate))

    def await_greetings(self, paired):
        barrier = pltpu.get_barrier_semaphore()

        ends = jnp.where(self.a > 0, 1, 0) + jnp.where(self.a < self.lines - 1, 1, 0)
        pl.semaphore_wait(barrier, ends + self.crosses + (1 if paired else 0))

    def ring(self, t):
        if t == 0:
            return [(self.a, 0, None)]
        up, down = self.a + t, self.a - t
        return [(down, -1, down >= 0), (up, 1, up < self.lines)]


def only(flag, action):
    if flag is None:
        action()
    else:
        pl.when(flag)(action)


def both(left, right):
    if left is None:
        return right
    return left if right is None else jnp.logical_and(left, right)


def split_rows(rows):
    alone = rows * 3 // 8
    return rows - alone, alone


def gather_kernel(lines, crosses, paired, *refs):
    count = len(paired)
    owns, outs = refs[:count], refs[count : 2 * count]
    sems = refs[2 * count : 3 * count]
    local_sem = refs[3 * count]
    here = Place(lines, crosses)
    pieces = lines * crosses
    zs0, zr0 = 0, 2 * lines
    xs0 = 3 * lines
    xr0, ys0, yr0, cs0, cr0 = (xs0 + k * pieces for k in range(1, 6))
    any_pair = any(paired)

    def span(item, p, q, c, part):
        rows = owns[item].shape[0]
        start = ((p * crosses + q) * 2 + c) * rows
        if part == "whole" or not paired[item]:
            return outs[item].at[pl.ds(pl.multiple_of(start, 16), rows)]
        carried, alone = split_rows(rows)
        if part == "carried":
            return outs[item].at[
                pl.ds(pl.multiple_of(start + alone * here.side, 16), carried)
            ]
        side = here.side if part == "mine" else 1 - here.side
        return outs[item].at[
            pl.ds(pl.multiple_of(start + carried * side, 16), alone)
        ]

    def move(item, ref, send, recv, device):
        return pltpu.make_async_remote_copy(
            src_ref=ref,
            dst_ref=ref,
            send_sem=sems[item].at[send],
            recv_sem=sems[item].at[recv],
            device_id=device,
            device_id_type=MESH,
        )

    def along(item, p, step):
        return move(
            item, span(item, p, here.b, here.c, "carried"),
            zs0 + 2 * p + (1 if step > 0 else 0), zr0 + p, here.at(a=here.a + step),
        )

    def across(item, p, q):
        return move(
            item, span(item, p, here.b, here.c, "carried"),
            xs0 + p * crosses + q, xr0 + p * crosses + here.b, here.at(b=q),
        )

    def crossed(item, p, q):
        return move(
            item, span(item, p, q, here.c, "carried"),
            xs0 + p * crosses + q, xr0 + p * crosses + q, here.at(b=q),
        )

    def to_mate(item, p, q, part="mine"):
        return move(
            item, span(item, p, q, here.c, part),
            ys0 + p * crosses + q, yr0 + p * crosses + q, here.at(dp=here.mate),
        )

    def to_core(item, p, q, c):
        return move(
            item, span(item, p, q, c, "whole"),
            cs0 + p * crosses + q, cr0 + p * crosses + q, here.at(c=1 - here.c),
        )

    def pass_on(item, p, q):
        if paired[item]:
            to_mate(item, p, q).start()
        else:
            to_core(item, p, q, here.c).start()

    here.greet(any_pair)
    copies = [
        pltpu.make_async_copy(
            owns[item], span(item, here.a, here.b, here.c, "whole"), local_sem.at[item]
        )
        for item in range(count)
    ]
    for copy in copies:
        copy.start()
    for copy in copies:
        copy.wait()
    here.await_greetings(any_pair)

    up_ok, down_ok = here.a < lines - 1, here.a > 0

    def send_line(item, p, step):
        only(up_ok if step > 0 else down_ok, lambda: along(item, p, step).start())

    for item in range(count):
        send_line(item, here.a, 1)
        send_line(item, here.a, -1)
        for q in here.others():
            across(item, here.a, q).start()
        to_core(item, here.a, here.b, here.c).start()

    def take_across(t):
        for p, _, ok in here.ring(t):

            def action(p=p):
                for item in range(count):
                    for q in here.others():
                        crossed(item, p, q).wait_recv()
                        pass_on(item, p, q)

            only(ok, action)

    def take_mate(t):
        for p, _, ok in here.ring(t):

            def action(p=p):
                for item in range(count):
                    if paired[item]:
                        for q in here.others() + ([] if t == 0 else [here.b]):
                            to_mate(item, p, q, "theirs").wait_recv()
                            to_core(item, p, q, here.c).start()

            only(ok, action)

    for t in range(1, lines):
        for p, step, ok in here.ring(t):

            def action(p=p, step=step):
                for item in range(count):
                    along(item, p, -step).wait_recv()
                    send_line(item, p, -step)
                    for q in here.others():
                        across(item, p, q).start()
                    pass_on(item, p, here.b)

            only(ok, action)
        take_across(t - 1)
        if t >= 2:
            take_mate(t - 2)
    take_across(lines - 1)
    if lines >= 2:
        take_mate(lines - 2)
    take_mate(lines - 1)

    for p in range(lines):
        for q in range(crosses):
            for item in range(count):
                to_core(item, p, q, 1 - here.c).wait_recv()
                to_core(item, p, q, here.c).wait_send()
                if paired[item]:
                    pl.when(jnp.logical_or(p != here.a, q != here.b))(
                        lambda item=item, p=p, q=q: to_mate(item, p, q).wait_send()
                    )
    for p in range(lines):
        for item in range(count):
            for q in here.others():
                across(item, p, q).wait_send()
            pl.when(jnp.logical_and(up_ok, p <= here.a))(
                lambda item=item, p=p: along(item, p, 1).wait_send()
            )
            pl.when(jnp.logical_and(down_ok, p >= here.a))(
                lambda item=item, p=p: along(item, p, -1).wait_send()
            )


def layout(size):
    lines = 4 if size % 8 == 0 else 1
    return lines, size // (2 * lines)


def gather(arrays, paired, size, collective_id):
    lines, crosses = layout(size)
    count = len(arrays)
    return pl.pallas_call(
        functools.partial(gather_kernel, lines, crosses, tuple(paired)),
        out_shape=[
            jax.ShapeDtypeStruct((size * x.shape[0],) + x.shape[1:], x.dtype) for x in arrays
        ],
        in_specs=[pl.BlockSpec(memory_space=pl.ANY)] * count,
        out_specs=[pl.BlockSpec(memory_space=pl.ANY)] * count,
        scratch_shapes=[
            pltpu.SemaphoreType.DMA((3 * lines + 6 * lines * crosses,)) for _ in range(count)
        ]
        + [pltpu.SemaphoreType.DMA((count,))],
        compiler_params=pltpu.CompilerParams(
            collective_id=collective_id, has_side_effects=True
        ),
    )(*arrays)


class Share:
    def __init__(self, here, paired, source, out_ref, scratch):
        self.here, self.paired, self.source, self.out = here, paired, source, out_ref
        self.sent, self.total, self.core_in, self.mate_in, self.cross_in, self.line_in = scratch[:6]
        self.last_in, self.sems = scratch[6:]
        lines, self.crosses = here.lines, here.crosses
        pieces = lines * self.crosses
        self.rows = rows = out_ref.shape[0]
        self.alone = alone = rows // 4 if paired else 0
        self.carried = carried = rows - alone
        self.base = [k * pieces for k in range(6)]
        self.zs0 = 6 * pieces
        self.zr0, self.fs = self.zs0 + lines, self.zs0 + 3 * lines
        self.first = pl.ds(0, rows)
        if paired:
            self.first = pl.ds(pl.multiple_of(alone * here.side, 16), carried)
            self.mine = pl.ds(pl.multiple_of(carried * here.side, 16), alone)
            self.theirs = pl.ds(pl.multiple_of(carried * (1 - here.side), 16), alone)

    def move(self, src, dst, send, recv, device):
        return pltpu.make_async_remote_copy(
            src_ref=src, dst_ref=dst, send_sem=self.sems.at[send], recv_sem=self.sems.at[recv],
            device_id=device, device_id_type=MESH,
        )

    def slot(self, p, q):
        return p * self.crosses + q

    def term(self, p, q, c):
        start = pl.multiple_of(((p * self.crosses + q) * 2 + c) * self.rows, self.rows)
        if len(self.source) == 1:
            return self.source[0][pl.ds(start, self.rows)]
        acts, grads = self.source
        return contract_first(acts[:, pl.ds(start, self.rows)], grads[...]).astype(jnp.bfloat16)

    def to_core(self, p, q):
        k = self.slot(p, q)
        return self.move(self.sent.at[k], self.core_in.at[k], self.base[0] + k,
                         self.base[1] + k, self.here.at(c=1 - self.here.c))

    def to_mate(self, p, q):
        k = self.slot(p, q)
        return self.move(self.total.at[k, self.theirs], self.mate_in.at[k], self.base[2] + k,
                         self.base[3] + k, self.here.at(dp=self.here.mate))

    def across(self, p, q):
        k = self.slot(p, self.here.b)
        return self.move(self.total.at[self.slot(p, q), self.first], self.cross_in.at[k],
                         self.base[4] + self.slot(p, q), self.base[5] + k, self.here.at(b=q))

    def crossed(self, p, q):
        k = self.slot(p, q)
        return self.move(self.total.at[k, self.first], self.cross_in.at[k],
                         self.base[4] + k, self.base[5] + k, self.here.at(b=q))

    def along(self, p, step):
        k = 2 * p + (0 if step > 0 else 1)
        return self.move(self.total.at[self.slot(p, self.here.b), self.first],
                         self.line_in.at[k], self.zs0 + p, self.zr0 + k,
                         self.here.at(a=self.here.a + step))

    def final(self):
        k = self.slot(self.here.a, self.here.b)
        return self.move(self.total.at[k, self.first], self.last_in, self.fs, self.fs + 1,
                         self.here.at(dp=self.here.mate))

    def begin(self, p, q):
        self.sent[self.slot(p, q)] = self.term(p, q, 1 - self.here.c)
        self.to_core(p, q).start()

    def join(self, p, q):
        k = self.slot(p, q)
        self.total[k] = self.term(p, q, self.here.c)
        self.to_core(p, q).wait_recv()
        self.total[k] = self.total[k] + self.core_in[k]
        if self.paired:
            self.to_mate(p, q).start()

    def cross(self, p, q, leave):
        k = self.slot(p, q)
        if self.paired:
            self.to_mate(p, q).wait_recv()
            self.total[k, self.mine] = self.total[k, self.mine] + self.mate_in[k]
        if leave:
            self.across(p, q).start()

    def run(self, p, step):
        here, k, first = self.here, self.slot(p, self.here.b), self.first
        for q in here.others():
            self.crossed(p, q).wait_recv()
            self.total[k, first] = self.total[k, first] + self.cross_in[self.slot(p, q)]

        def add(side):
            self.along(p, 1 if side == 0 else -1).wait_recv()
            self.total[k, first] = self.total[k, first] + self.line_in[2 * p + side]

        if step >= 0:
            pl.when(here.a > 0)(lambda: add(0))
        if step <= 0:
            pl.when(here.a < here.lines - 1)(lambda: add(1))
        if step != 0:
            self.along(p, step).start()
        elif self.paired:
            self.final().start()

    def finish(self):
        here, kind = self.here, self.out.dtype
        k = self.slot(here.a, here.b)
        if not self.paired:
            self.out[...] = self.total[k].astype(kind)
            return
        alone, carried = self.alone, self.carried
        middle = carried - alone
        self.final().wait_recv()
        self.out[self.mine] = self.total[k, self.mine].astype(kind)
        their_at = pl.multiple_of(middle * (1 - here.side), 16)
        self.out[self.theirs] = self.last_in[pl.ds(their_at, alone)].astype(kind)
        shared_at = pl.multiple_of(alone * here.side, 16)
        self.out[pl.ds(alone, middle)] = self.total[k, pl.ds(alone, middle)].astype(
            kind
        ) + self.last_in[pl.ds(shared_at, middle)].astype(kind)
        self.final().wait_send()

    def drain(self):
        here = self.here
        for p in range(here.lines):
            for q in range(self.crosses):
                self.to_core(p, q).wait_send()
                if self.paired:
                    self.to_mate(p, q).wait_send()
            for q in here.others():
                self.across(p, q).wait_send()
            pl.when(p > here.a)(lambda p=p: self.along(p, 1).wait_send())
            pl.when(p < here.a)(lambda p=p: self.along(p, -1).wait_send())


def reduce_kernel(lines, crosses, forms, *refs):
    here = Place(lines, crosses)
    refs, sources = list(refs), []
    for inputs, _ in forms:
        sources.append(refs[:inputs])
        refs = refs[inputs:]
    outs, refs = refs[: len(forms)], refs[len(forms) :]
    shares = [
        Share(here, paired, sources[k], outs[k], refs[8 * k : 8 * k + 8])
        for k, (_, paired) in enumerate(forms)
    ]
    any_pair = any(paired for _, paired in forms)
    here.greet(any_pair)
    here.await_greetings(any_pair)

    def each(t, action):
        if 0 <= t < lines:
            for p, step, ok in here.ring(t):

                def apply(p=p, step=step):
                    for share in shares:
                        action(share, p, step)

                only(ok, apply)

    for t in range(lines - 1, -1, -1):
        for q in here.others() + [here.b]:
            each(t, lambda share, p, step, q=q: share.begin(p, q))
    for t in range(lines - 1, -3, -1):
        for q in here.others() + [here.b]:
            each(t, lambda share, p, step, q=q: share.join(p, q))
        for q in here.others():
            each(t + 1, lambda share, p, step, q=q: share.cross(p, q, True))
        each(t + 1, lambda share, p, step: share.cross(p, here.b, False))
        each(t + 2, lambda share, p, step: share.run(p, step))
    for share in shares:
        share.finish()
    for share in shares:
        share.drain()


def reduce_scatter(sources, paired, out_dtypes, size, collective_id):
    lines, crosses = layout(size)
    pieces = lines * crosses
    kind = jnp.bfloat16
    outs, scratch = [], []
    for source, pair, out_dtype in zip(sources, paired, out_dtypes):
        rows = source[0].shape[len(source) - 1] // size
        width = source[-1].shape[1]
        alone = rows // 4 if pair else 16
        carried = rows - rows // 4 if pair else rows
        outs.append(jax.ShapeDtypeStruct((rows, width), out_dtype))
        scratch += [
            pltpu.VMEM((pieces, rows, width), kind),
            pltpu.VMEM((pieces, rows, width), kind),
            pltpu.VMEM((pieces, rows, width), kind),
            pltpu.VMEM((pieces, alone, width), kind),
            pltpu.VMEM((pieces, carried, width), kind),
            pltpu.VMEM((2 * lines, carried, width), kind),
            pltpu.VMEM((carried, width), kind),
            pltpu.SemaphoreType.DMA((6 * pieces + 3 * lines + 2,)),
        ]
    flat = [x for source in sources for x in source]
    forms = tuple((len(source), pair) for source, pair in zip(sources, paired))
    return pl.pallas_call(
        functools.partial(reduce_kernel, lines, crosses, forms),
        out_shape=outs,
        in_specs=[pl.BlockSpec(memory_space=pltpu.VMEM)] * len(flat),
        out_specs=[pl.BlockSpec(memory_space=pltpu.VMEM)] * len(outs),
        scratch_shapes=scratch,
        compiler_params=pltpu.CompilerParams(
            collective_id=collective_id, has_side_effects=True,
            vmem_limit_bytes=48 * 1024 * 1024,
        ),
    )(*flat)


def expert_gates(scores, chosen, experts):
    chosen_hit = chosen[:, :, None] == lax.iota(jnp.int32, experts)[None, None, :]
    return jnp.where(jnp.any(chosen_hit, axis=1), scores, jnp.float32(0.0))


def contract_last(left, right):
    return lax.dot_general(
        left, right, (((1,), (1,)), ((), ())), preferred_element_type=jnp.float32
    )


def contract_first(left, right):
    return lax.dot_general(
        left, right, (((0,), (0,)), ((), ())), preferred_element_type=jnp.float32
    )


def body(
    tokens,
    queries,
    key_vectors,
    doc_position,
    value_scores,
    value_experts,
    output_scores,
    output_experts,
    value_panels,
    output_panels,
    cotangent,
):
    tok_block = tokens[0]
    query_block = queries[0]
    own_keys = key_vectors[0]
    positions = doc_position[0]
    grad_rows = cotangent[0]
    tok_rows = tok_block.shape[0]
    head_size = query_block.shape[1]
    experts = value_scores.shape[2]
    panel_width = value_panels.shape[1]
    value_gate = expert_gates(value_scores[0], value_experts[0], experts)
    output_gate = expert_gates(output_scores[0], output_experts[0], experts)
    size = lax.axis_size("seq")
    pair_count = lax.axis_size("dp")
    value_full, keys_all = gather([value_panels, own_keys], [True, False], size, 0)
    projection = jnp.dot(tok_block, value_full, preferred_element_type=jnp.float32)
    value_vec = jnp.sum(
        projection.reshape(tok_rows, experts, head_size) * value_gate[:, :, None], axis=1
    ).astype(jnp.bfloat16)
    values_all, output_full = gather([value_vec, output_panels], [False, True], size, 1)
    length = keys_all.shape[0]
    score_scale = head_size ** (-0.5)
    query_index = lax.axis_index("seq") * tok_rows + lax.iota(jnp.int32, tok_rows)
    key_index = lax.iota(jnp.int32, length)
    visible = (key_index[None, :] <= query_index[:, None]) & (
        query_index[:, None] - key_index[None, :] <= positions[:, None]
    )
    masked = jnp.where(visible, contract_last(query_block, keys_all) * score_scale, -jnp.inf)
    row_max = jnp.max(masked, axis=1)
    log_total = row_max + jnp.log(jnp.sum(jnp.exp(masked - row_max[:, None]), axis=1))
    attn_prob = jnp.exp(masked - log_total[:, None])
    prob_low = attn_prob.astype(jnp.bfloat16)
    attended = jnp.dot(prob_low, values_all, preferred_element_type=jnp.float32).astype(
        jnp.bfloat16
    )
    expanded = (
        (output_gate[:, :, None] * attended.astype(jnp.float32)[:, None, :])
        .reshape(tok_rows, panel_width)
        .astype(jnp.bfloat16)
    )
    layer_output = contract_last(expanded, output_full).astype(jnp.bfloat16)
    pulled = jnp.dot(grad_rows, output_full, preferred_element_type=jnp.float32)
    dattended = jnp.sum(
        pulled.reshape(tok_rows, experts, head_size) * output_gate[:, :, None], axis=1
    ).astype(jnp.bfloat16)
    row_delta = jnp.sum(dattended.astype(jnp.float32) * attended.astype(jnp.float32), axis=1)
    dweights = contract_last(dattended, values_all)
    dscores = (attn_prob * (dweights - row_delta[:, None])).astype(jnp.bfloat16)
    grad_queries = (
        jnp.dot(dscores, keys_all, preferred_element_type=jnp.float32) * score_scale
    ).astype(jnp.bfloat16)
    key_term = contract_first(dscores, query_block) * score_scale
    value_term = contract_first(prob_low, dattended)
    own_sums, grad_output = reduce_scatter(
        [
            (jnp.concatenate([key_term, value_term], axis=1).astype(jnp.bfloat16),),
            (grad_rows, expanded),
        ],
        [False, True], [jnp.bfloat16, jnp.float32], size, 2,
    )
    grad_keys, dvalue = own_sums[:, :head_size], own_sums[:, head_size:]
    value_grad = (
        (value_gate[:, :, None] * dvalue.astype(jnp.float32)[:, None, :])
        .reshape(tok_rows, panel_width)
        .astype(jnp.bfloat16)
    )
    grad_tokens = contract_last(value_grad, value_full).astype(jnp.bfloat16)
    (grad_value,) = reduce_scatter(
        [(tok_block, value_grad)], [True], [jnp.float32], size, 3
    )
    if pair_count > 2:
        grad_value, grad_output = lax.psum((grad_value * 0.5, grad_output * 0.5), "dp")
    return (
        layer_output[None],
        grad_tokens[None],
        grad_queries[None],
        grad_keys[None],
        grad_value,
        grad_output,
    )


def solution(mesh):
    in_specs = (
        P("dp", "seq", None),
        P("dp", "seq", None),
        P("dp", "seq", None),
        P("dp", "seq"),
        P("dp", "seq", None),
        P("dp", "seq", None),
        P("dp", "seq", None),
        P("dp", "seq", None),
        P("seq", None),
        P("seq", None),
        P("dp", "seq", None),
    )
    out_specs = (
        P("dp", "seq", None),
        P("dp", "seq", None),
        P("dp", "seq", None),
        P("dp", "seq", None),
        P("seq", None),
        P("seq", None),
    )
    return jax.shard_map(body, mesh=mesh, in_specs=in_specs, out_specs=out_specs, check_vma=False)
```

```python
import functools

import jax
import jax.numpy as jnp
from jax import lax
from jax.experimental import pallas as pl
from jax.experimental.pallas import tpu as pltpu
from jax.sharding import PartitionSpec as P

MESH = pl.DeviceIdType.MESH


class Place:
    def __init__(self, lines, crosses):
        index = lax.axis_index("seq")
        self.lines, self.crosses = lines, crosses
        self.dp = lax.axis_index("dp")
        self.a = index // (2 * crosses)
        self.b = (index // 2) % crosses
        self.c = index % 2
        self.side = self.dp % 2
        self.mate = self.dp + 1 - 2 * self.side

    def at(self, a=None, b=None, c=None, dp=None):
        a = self.a if a is None else a
        b = self.b if b is None else b
        c = self.c if c is None else c
        dp = self.dp if dp is None else dp
        return (dp, (a * self.crosses + b) * 2 + c)

    def others(self):
        return [lax.rem(self.b + k, self.crosses) for k in range(1, self.crosses)]

    def greet(self, paired):
        barrier = pltpu.get_barrier_semaphore()

        def hail(device):
            pl.semaphore_signal(barrier, inc=1, device_id=device, device_id_type=MESH)

        @pl.when(self.a > 0)
        def _():
            hail(self.at(a=self.a - 1))

        @pl.when(self.a < self.lines - 1)
        def _():
            hail(self.at(a=self.a + 1))

        for q in self.others():
            hail(self.at(b=q))
        hail(self.at(c=1 - self.c))
        if paired:
            hail(self.at(dp=self.mate))

    def await_greetings(self, paired):
        barrier = pltpu.get_barrier_semaphore()

        ends = jnp.where(self.a > 0, 1, 0) + jnp.where(self.a < self.lines - 1, 1, 0)
        pl.semaphore_wait(barrier, ends + self.crosses + (1 if paired else 0))

    def ring(self, t):
        if t == 0:
            return [(self.a, 0, None)]
        up, down = self.a + t, self.a - t
        return [(down, -1, down >= 0), (up, 1, up < self.lines)]


def only(flag, action):
    if flag is None:
        action()
    else:
        pl.when(flag)(action)


def both(left, right):
    if left is None:
        return right
    return left if right is None else jnp.logical_and(left, right)


def split_rows(rows):
    alone = rows * 3 // 8
    return rows - alone, alone


def gather_kernel(lines, crosses, paired, *refs):
    count = len(paired)
    owns, outs = refs[:count], refs[count : 2 * count]
    sems = refs[2 * count : 3 * count]
    local_sem = refs[3 * count]
    here = Place(lines, crosses)
    pieces = lines * crosses
    zs0, zr0 = 0, 2 * lines
    xs0 = 3 * lines
    xr0, ys0, yr0, cs0, cr0 = (xs0 + k * pieces for k in range(1, 6))
    any_pair = any(paired)

    def span(item, p, q, c, part):
        rows = owns[item].shape[0]
        start = ((p * crosses + q) * 2 + c) * rows
        if part == "whole" or not paired[item]:
            return outs[item].at[pl.ds(pl.multiple_of(start, 16), rows)]
        carried, alone = split_rows(rows)
        if part == "carried":
            return outs[item].at[
                pl.ds(pl.multiple_of(start + alone * here.side, 16), carried)
            ]
        side = here.side if part == "mine" else 1 - here.side
        return outs[item].at[
            pl.ds(pl.multiple_of(start + carried * side, 16), alone)
        ]

    def move(item, ref, send, recv, device):
        return pltpu.make_async_remote_copy(
            src_ref=ref,
            dst_ref=ref,
            send_sem=sems[item].at[send],
            recv_sem=sems[item].at[recv],
            device_id=device,
            device_id_type=MESH,
        )

    def along(item, p, step):
        return move(
            item, span(item, p, here.b, here.c, "carried"),
            zs0 + 2 * p + (1 if step > 0 else 0), zr0 + p, here.at(a=here.a + step),
        )

    def across(item, p, q):
        return move(
            item, span(item, p, here.b, here.c, "carried"),
            xs0 + p * crosses + q, xr0 + p * crosses + here.b, here.at(b=q),
        )

    def crossed(item, p, q):
        return move(
            item, span(item, p, q, here.c, "carried"),
            xs0 + p * crosses + q, xr0 + p * crosses + q, here.at(b=q),
        )

    def to_mate(item, p, q, part="mine"):
        return move(
            item, span(item, p, q, here.c, part),
            ys0 + p * crosses + q, yr0 + p * crosses + q, here.at(dp=here.mate),
        )

    def to_core(item, p, q, c):
        return move(
            item, span(item, p, q, c, "whole"),
            cs0 + p * crosses + q, cr0 + p * crosses + q, here.at(c=1 - here.c),
        )

    def pass_on(item, p, q):
        if paired[item]:
            to_mate(item, p, q).start()
        else:
            to_core(item, p, q, here.c).start()

    here.greet(any_pair)
    copies = [
        pltpu.make_async_copy(
            owns[item], span(item, here.a, here.b, here.c, "whole"), local_sem.at[item]
        )
        for item in range(count)
    ]
    for copy in copies:
        copy.start()
    for copy in copies:
        copy.wait()
    here.await_greetings(any_pair)

    up_ok, down_ok = here.a < lines - 1, here.a > 0

    def send_line(item, p, step):
        only(up_ok if step > 0 else down_ok, lambda: along(item, p, step).start())

    for item in range(count):
        send_line(item, here.a, 1)
        send_line(item, here.a, -1)
        for q in here.others():
            across(item, here.a, q).start()
        to_core(item, here.a, here.b, here.c).start()

    def take_across(t):
        for p, _, ok in here.ring(t):

            def action(p=p):
                for item in range(count):
                    for q in here.others():
                        crossed(item, p, q).wait_recv()
                        pass_on(item, p, q)

            only(ok, action)

    def take_mate(t):
        for p, _, ok in here.ring(t):

            def action(p=p):
                for item in range(count):
                    if paired[item]:
                        for q in here.others() + ([] if t == 0 else [here.b]):
                            to_mate(item, p, q, "theirs").wait_recv()
                            to_core(item, p, q, here.c).start()

            only(ok, action)

    for t in range(1, lines):
        for p, step, ok in here.ring(t):

            def action(p=p, step=step):
                for item in range(count):
                    along(item, p, -step).wait_recv()
                    send_line(item, p, -step)
                    for q in here.others():
                        across(item, p, q).start()
                    pass_on(item, p, here.b)

            only(ok, action)
        take_across(t - 1)
        if t >= 2:
            take_mate(t - 2)
    take_across(lines - 1)
    if lines >= 2:
        take_mate(lines - 2)
    take_mate(lines - 1)

    for p in range(lines):
        for q in range(crosses):
            for item in range(count):
                to_core(item, p, q, 1 - here.c).wait_recv()
                to_core(item, p, q, here.c).wait_send()
                if paired[item]:
                    pl.when(jnp.logical_or(p != here.a, q != here.b))(
                        lambda item=item, p=p, q=q: to_mate(item, p, q).wait_send()
                    )
    for p in range(lines):
        for item in range(count):
            for q in here.others():
                across(item, p, q).wait_send()
            pl.when(jnp.logical_and(up_ok, p <= here.a))(
                lambda item=item, p=p: along(item, p, 1).wait_send()
            )
            pl.when(jnp.logical_and(down_ok, p >= here.a))(
                lambda item=item, p=p: along(item, p, -1).wait_send()
            )


def layout(size):
    lines = 4 if size % 8 == 0 else 1
    return lines, size // (2 * lines)


def gather(arrays, paired, size, collective_id):
    lines, crosses = layout(size)
    count = len(arrays)
    return pl.pallas_call(
        functools.partial(gather_kernel, lines, crosses, tuple(paired)),
        out_shape=[
            jax.ShapeDtypeStruct((size * x.shape[0],) + x.shape[1:], x.dtype) for x in arrays
        ],
        in_specs=[pl.BlockSpec(memory_space=pltpu.VMEM)] * count,
        out_specs=[pl.BlockSpec(memory_space=pltpu.VMEM)] * count,
        scratch_shapes=[
            pltpu.SemaphoreType.DMA((3 * lines + 6 * lines * crosses,)) for _ in range(count)
        ]
        + [pltpu.SemaphoreType.DMA((count,))],
        compiler_params=pltpu.CompilerParams(
            collective_id=collective_id, has_side_effects=True,
            vmem_limit_bytes=32 * 1024 * 1024,
        ),
    )(*arrays)


class Share:
    def __init__(self, here, paired, source, out_ref, scratch):
        self.here, self.paired, self.source, self.out = here, paired, source, out_ref
        self.sent, self.total, self.core_in, self.mate_in, self.cross_in, self.line_in = scratch[:6]
        self.last_in, self.sems = scratch[6:]
        lines, self.crosses = here.lines, here.crosses
        pieces = lines * self.crosses
        self.rows = rows = out_ref.shape[0]
        self.alone = alone = rows // 4 if paired else 0
        self.carried = carried = rows - alone
        self.base = [k * pieces for k in range(6)]
        self.zs0 = 6 * pieces
        self.zr0, self.fs = self.zs0 + lines, self.zs0 + 3 * lines
        self.first = pl.ds(0, rows)
        if paired:
            self.first = pl.ds(pl.multiple_of(alone * here.side, 16), carried)
            self.mine = pl.ds(pl.multiple_of(carried * here.side, 16), alone)
            self.theirs = pl.ds(pl.multiple_of(carried * (1 - here.side), 16), alone)

    def move(self, src, dst, send, recv, device):
        return pltpu.make_async_remote_copy(
            src_ref=src, dst_ref=dst, send_sem=self.sems.at[send], recv_sem=self.sems.at[recv],
            device_id=device, device_id_type=MESH,
        )

    def slot(self, p, q):
        return p * self.crosses + q

    def term(self, p, q, c):
        start = pl.multiple_of(((p * self.crosses + q) * 2 + c) * self.rows, self.rows)
        if len(self.source) == 1:
            return self.source[0][pl.ds(start, self.rows)]
        acts, grads = self.source
        return contract_first(acts[:, pl.ds(start, self.rows)], grads[...]).astype(jnp.bfloat16)

    def to_core(self, p, q):
        k = self.slot(p, q)
        return self.move(self.sent.at[k], self.core_in.at[k], self.base[0] + k,
                         self.base[1] + k, self.here.at(c=1 - self.here.c))

    def to_mate(self, p, q):
        k = self.slot(p, q)
        return self.move(self.total.at[k, self.theirs], self.mate_in.at[k], self.base[2] + k,
                         self.base[3] + k, self.here.at(dp=self.here.mate))

    def across(self, p, q):
        k = self.slot(p, self.here.b)
        return self.move(self.total.at[self.slot(p, q), self.first], self.cross_in.at[k],
                         self.base[4] + self.slot(p, q), self.base[5] + k, self.here.at(b=q))

    def crossed(self, p, q):
        k = self.slot(p, q)
        return self.move(self.total.at[k, self.first], self.cross_in.at[k],
                         self.base[4] + k, self.base[5] + k, self.here.at(b=q))

    def along(self, p, step):
        k = 2 * p + (0 if step > 0 else 1)
        return self.move(self.total.at[self.slot(p, self.here.b), self.first],
                         self.line_in.at[k], self.zs0 + p, self.zr0 + k,
                         self.here.at(a=self.here.a + step))

    def final(self):
        k = self.slot(self.here.a, self.here.b)
        return self.move(self.total.at[k, self.first], self.last_in, self.fs, self.fs + 1,
                         self.here.at(dp=self.here.mate))

    def begin(self, p, q):
        self.sent[self.slot(p, q)] = self.term(p, q, 1 - self.here.c)
        self.to_core(p, q).start()

    def join(self, p, q):
        k = self.slot(p, q)
        self.total[k] = self.term(p, q, self.here.c)
        self.to_core(p, q).wait_recv()
        self.total[k] = self.total[k] + self.core_in[k]
        if self.paired:
            self.to_mate(p, q).start()

    def cross(self, p, q, leave):
        k = self.slot(p, q)
        if self.paired:
            self.to_mate(p, q).wait_recv()
            self.total[k, self.mine] = self.total[k, self.mine] + self.mate_in[k]
        if leave:
            self.across(p, q).start()

    def run(self, p, step):
        here, k, first = self.here, self.slot(p, self.here.b), self.first
        for q in here.others():
            self.crossed(p, q).wait_recv()
            self.total[k, first] = self.total[k, first] + self.cross_in[self.slot(p, q)]

        def add(side):
            self.along(p, 1 if side == 0 else -1).wait_recv()
            self.total[k, first] = self.total[k, first] + self.line_in[2 * p + side]

        if step >= 0:
            pl.when(here.a > 0)(lambda: add(0))
        if step <= 0:
            pl.when(here.a < here.lines - 1)(lambda: add(1))
        if step != 0:
            self.along(p, step).start()
        elif self.paired:
            self.final().start()

    def finish(self):
        here, kind = self.here, self.out.dtype
        k = self.slot(here.a, here.b)
        if not self.paired:
            self.out[...] = self.total[k].astype(kind)
            return
        alone, carried = self.alone, self.carried
        middle = carried - alone
        self.final().wait_recv()
        self.out[self.mine] = self.total[k, self.mine].astype(kind)
        their_at = pl.multiple_of(middle * (1 - here.side), 16)
        self.out[self.theirs] = self.last_in[pl.ds(their_at, alone)].astype(kind)
        shared_at = pl.multiple_of(alone * here.side, 16)
        self.out[pl.ds(alone, middle)] = self.total[k, pl.ds(alone, middle)].astype(
            kind
        ) + self.last_in[pl.ds(shared_at, middle)].astype(kind)
        self.final().wait_send()

    def drain(self):
        here = self.here
        for p in range(here.lines):
            for q in range(self.crosses):
                self.to_core(p, q).wait_send()
                if self.paired:
                    self.to_mate(p, q).wait_send()
            for q in here.others():
                self.across(p, q).wait_send()
            pl.when(p > here.a)(lambda p=p: self.along(p, 1).wait_send())
            pl.when(p < here.a)(lambda p=p: self.along(p, -1).wait_send())


def reduce_kernel(lines, crosses, forms, *refs):
    here = Place(lines, crosses)
    refs, sources = list(refs), []
    for inputs, _ in forms:
        sources.append(refs[:inputs])
        refs = refs[inputs:]
    outs, refs = refs[: len(forms)], refs[len(forms) :]
    shares = [
        Share(here, paired, sources[k], outs[k], refs[8 * k : 8 * k + 8])
        for k, (_, paired) in enumerate(forms)
    ]
    any_pair = any(paired for _, paired in forms)
    here.greet(any_pair)
    here.await_greetings(any_pair)

    def each(t, action):
        if 0 <= t < lines:
            for p, step, ok in here.ring(t):

                def apply(p=p, step=step):
                    for share in shares:
                        action(share, p, step)

                only(ok, apply)

    for t in range(lines - 1, -1, -1):
        for q in here.others() + [here.b]:
            each(t, lambda share, p, step, q=q: share.begin(p, q))
    for t in range(lines - 1, -3, -1):
        for q in here.others() + [here.b]:
            each(t, lambda share, p, step, q=q: share.join(p, q))
        for q in here.others():
            each(t + 1, lambda share, p, step, q=q: share.cross(p, q, True))
        each(t + 1, lambda share, p, step: share.cross(p, here.b, False))
        each(t + 2, lambda share, p, step: share.run(p, step))
    for share in shares:
        share.finish()
    for share in shares:
        share.drain()


def reduce_scatter(sources, paired, out_dtypes, size, collective_id):
    lines, crosses = layout(size)
    pieces = lines * crosses
    kind = jnp.bfloat16
    outs, scratch = [], []
    for source, pair, out_dtype in zip(sources, paired, out_dtypes):
        rows = source[0].shape[len(source) - 1] // size
        width = source[-1].shape[1]
        alone = rows // 4 if pair else 16
        carried = rows - rows // 4 if pair else rows
        outs.append(jax.ShapeDtypeStruct((rows, width), out_dtype))
        scratch += [
            pltpu.VMEM((pieces, rows, width), kind),
            pltpu.VMEM((pieces, rows, width), kind),
            pltpu.VMEM((pieces, rows, width), kind),
            pltpu.VMEM((pieces, alone, width), kind),
            pltpu.VMEM((pieces, carried, width), kind),
            pltpu.VMEM((2 * lines, carried, width), kind),
            pltpu.VMEM((carried, width), kind),
            pltpu.SemaphoreType.DMA((6 * pieces + 3 * lines + 2,)),
        ]
    flat = [x for source in sources for x in source]
    forms = tuple((len(source), pair) for source, pair in zip(sources, paired))
    return pl.pallas_call(
        functools.partial(reduce_kernel, lines, crosses, forms),
        out_shape=outs,
        in_specs=[pl.BlockSpec(memory_space=pltpu.VMEM)] * len(flat),
        out_specs=[pl.BlockSpec(memory_space=pltpu.VMEM)] * len(outs),
        scratch_shapes=scratch,
        compiler_params=pltpu.CompilerParams(
            collective_id=collective_id, has_side_effects=True,
            vmem_limit_bytes=48 * 1024 * 1024,
        ),
    )(*flat)


def expert_gates(scores, chosen, experts):
    chosen_hit = chosen[:, :, None] == lax.iota(jnp.int32, experts)[None, None, :]
    return jnp.where(jnp.any(chosen_hit, axis=1), scores, jnp.float32(0.0))


def contract_last(left, right):
    return lax.dot_general(
        left, right, (((1,), (1,)), ((), ())), preferred_element_type=jnp.float32
    )


def contract_first(left, right):
    return lax.dot_general(
        left, right, (((0,), (0,)), ((), ())), preferred_element_type=jnp.float32
    )


def body(
    tokens,
    queries,
    key_vectors,
    doc_position,
    value_scores,
    value_experts,
    output_scores,
    output_experts,
    value_panels,
    output_panels,
    cotangent,
):
    tok_block = tokens[0]
    query_block = queries[0]
    own_keys = key_vectors[0]
    positions = doc_position[0]
    grad_rows = cotangent[0]
    tok_rows = tok_block.shape[0]
    head_size = query_block.shape[1]
    experts = value_scores.shape[2]
    panel_width = value_panels.shape[1]
    value_gate = expert_gates(value_scores[0], value_experts[0], experts)
    output_gate = expert_gates(output_scores[0], output_experts[0], experts)
    size = lax.axis_size("seq")
    pair_count = lax.axis_size("dp")
    value_full, keys_all = gather([value_panels, own_keys], [True, False], size, 0)
    projection = jnp.dot(tok_block, value_full, preferred_element_type=jnp.float32)
    value_vec = jnp.sum(
        projection.reshape(tok_rows, experts, head_size) * value_gate[:, :, None], axis=1
    ).astype(jnp.bfloat16)
    values_all, output_full = gather([value_vec, output_panels], [False, True], size, 1)
    length = keys_all.shape[0]
    score_scale = head_size ** (-0.5)
    query_index = lax.axis_index("seq") * tok_rows + lax.iota(jnp.int32, tok_rows)
    key_index = lax.iota(jnp.int32, length)
    visible = (key_index[None, :] <= query_index[:, None]) & (
        query_index[:, None] - key_index[None, :] <= positions[:, None]
    )
    masked = jnp.where(visible, contract_last(query_block, keys_all) * score_scale, -jnp.inf)
    row_max = jnp.max(masked, axis=1)
    log_total = row_max + jnp.log(jnp.sum(jnp.exp(masked - row_max[:, None]), axis=1))
    attn_prob = jnp.exp(masked - log_total[:, None])
    prob_low = attn_prob.astype(jnp.bfloat16)
    attended = jnp.dot(prob_low, values_all, preferred_element_type=jnp.float32).astype(
        jnp.bfloat16
    )
    expanded = (
        (output_gate[:, :, None] * attended.astype(jnp.float32)[:, None, :])
        .reshape(tok_rows, panel_width)
        .astype(jnp.bfloat16)
    )
    layer_output = contract_last(expanded, output_full).astype(jnp.bfloat16)
    pulled = jnp.dot(grad_rows, output_full, preferred_element_type=jnp.float32)
    dattended = jnp.sum(
        pulled.reshape(tok_rows, experts, head_size) * output_gate[:, :, None], axis=1
    ).astype(jnp.bfloat16)
    row_delta = jnp.sum(dattended.astype(jnp.float32) * attended.astype(jnp.float32), axis=1)
    dweights = contract_last(dattended, values_all)
    dscores = (attn_prob * (dweights - row_delta[:, None])).astype(jnp.bfloat16)
    grad_queries = (
        jnp.dot(dscores, keys_all, preferred_element_type=jnp.float32) * score_scale
    ).astype(jnp.bfloat16)
    key_term = contract_first(dscores, query_block) * score_scale
    value_term = contract_first(prob_low, dattended)
    own_sums, grad_output = reduce_scatter(
        [
            (jnp.concatenate([key_term, value_term], axis=1).astype(jnp.bfloat16),),
            (grad_rows, expanded),
        ],
        [False, True], [jnp.bfloat16, jnp.float32], size, 2,
    )
    grad_keys, dvalue = own_sums[:, :head_size], own_sums[:, head_size:]
    value_grad = (
        (value_gate[:, :, None] * dvalue.astype(jnp.float32)[:, None, :])
        .reshape(tok_rows, panel_width)
        .astype(jnp.bfloat16)
    )
    grad_tokens = contract_last(value_grad, value_full).astype(jnp.bfloat16)
    (grad_value,) = reduce_scatter(
        [(tok_block, value_grad)], [True], [jnp.float32], size, 3
    )
    if pair_count > 2:
        grad_value, grad_output = lax.psum((grad_value * 0.5, grad_output * 0.5), "dp")
    return (
        layer_output[None],
        grad_tokens[None],
        grad_queries[None],
        grad_keys[None],
        grad_value,
        grad_output,
    )


def solution(mesh):
    in_specs = (
        P("dp", "seq", None),
        P("dp", "seq", None),
        P("dp", "seq", None),
        P("dp", "seq"),
        P("dp", "seq", None),
        P("dp", "seq", None),
        P("dp", "seq", None),
        P("dp", "seq", None),
        P("seq", None),
        P("seq", None),
        P("dp", "seq", None),
    )
    out_specs = (
        P("dp", "seq", None),
        P("dp", "seq", None),
        P("dp", "seq", None),
        P("dp", "seq", None),
        P("seq", None),
        P("seq", None),
    )
    return jax.shard_map(body, mesh=mesh, in_specs=in_specs, out_specs=out_specs, check_vma=False)
```
